512 devices in a mesh: mem: 8 (over z), lat: 32 (over y, x), rep: 2 (over core).
Axes of the slice: x: 4, y: 8, z: 8, core: 2. Of those that a mesh axis runs over, the one named last changes fastest.
Arguments:
- latent: bfloat16 [80, 16384, 256], P(('rep', 'mem'), 'lat'), parts along dimension 0, may hold values from -6 to 6
- in_weight: bfloat16 [256, 1024], replicated, may hold values from -0.375 to 0.375
- in_bias: float32 [1024], replicated, may hold values from -3 to 3
- out_weight: bfloat16 [4, 1024], replicated, may hold values from -0.1875 to 0.1875
- out_bias: float32 [4], replicated, may hold values from -3 to 3
- observed: float32 [8, 16384], P('rep', 'lat'), parts along dimension 0, may hold values from -6 to 6
- patch_of_cell: int32 [16384], P('lat'), may hold values from 0 to 7, as said below
Outputs:
- d_latent: bfloat16 [80, 16384, 256], P(('rep', 'mem'), 'lat'), parts along dimension 0
- d_in_weight: float32 [512, 1024], P('rep'), parts along dimension 0
- d_out_weight: float32 [8, 1024], P('rep'), parts along dimension 0
- d_in_bias: float32 [2048], P('rep'), parts along dimension 0
- d_out_bias: float32 [8], P('rep'), parts along dimension 0
The draws below stay inside these ranges and needn't reach their ends.
There are 2 independent parts, one for each index of `rep`. The reference program is written for one: setup_inputs(seed, part) draws one part's arguments, and reference() takes and returns one part's arrays. A program takes and returns all parts, laid end to end along the dimension named above; an argument that names none is the same for every part. Nothing has to cross between parts.
Inputs may be any that keep to these rules, and one draw needn't show every extreme that they name: `patch_of_cell`: each of the 8 patches holds exactly 2048 cells; patches 2 g and 2 g + 1 together hold exactly the cells 8 g * 512 to 8 (g + 1) * 512 - 1.
All inputs are finite; a program needn't handle non-finite values.
Results may differ from the reference program's by a relative error of at most 0.0025.
The reference program's roundings to bfloat16 on the way count: a program that leaves them out, or rounds other values in their place, can miss the bound.
Values may be sent and summed in bfloat16 or wider, within the bound.
No kernel may reach another device: no remote copies, remote signals or barrier semaphores. Data moves between devices by JAX's collectives and lax.ppermute only.
A program may use at most 64 MiB of HBM per device.

```python
import jax
import jax.numpy as jnp
from jax import lax

D = 256
HID = 1024
NVAR = 4
MEMBERS = 40
CELLS = 16384
PATCH = 2048
NPATCH = 8


def draw_patch_of_cell(key, part):
    key = jax.random.fold_in(key, 11)
    groups = CELLS // (2 * PATCH)
    keys = jax.random.split(key, groups)
    orders = jax.vmap(lambda single: jax.random.permutation(single, 2 * PATCH))(keys)
    second = (orders >= PATCH).astype(jnp.int32)
    patch_ids = 2 * jnp.arange(groups, dtype=jnp.int32)[:, None] + second
    return patch_ids.reshape(CELLS).astype(jnp.int32)


def block_levels(rng, shape, cuts, smallest, high):
    def one(position, blocks):
        draws = jax.random.uniform(jax.random.fold_in(jax.random.fold_in(rng, 6), position), (blocks,), jnp.float32, smallest / len(cuts), high / len(cuts))
        return jnp.repeat(jnp.exp(draws), shape[position] // blocks).reshape((-1,) + (1,) * (len(shape) - position - 1))

    gain = one(*cuts[0])
    for cut in cuts[1:]:
        gain = gain * one(*cut)
    return gain


def noise(rng, dims, width, limit, shards=(), kind=jnp.bfloat16):
    values = jax.random.normal(rng, dims, jnp.float32) * width
    if len(shards) > 0:
        values = block_levels(rng, dims, shards, -0.22, 0.18) * values
    return jnp.clip(values, min=-limit, max=limit).astype(kind)


def setup_inputs(seed: int = 0, part: int = 0) -> dict:
    key_of = jax.random.split(jax.random.key(seed), 8)
    part_splits = jax.random.split(jax.random.fold_in(key_of[7], part), 8)
    latent = noise(part_splits[0], (MEMBERS, CELLS, D), 1.0, 6.0, ((0, 8), (1, 32)))
    in_weight = noise(key_of[1], (D, HID), D ** -0.5, 0.375)
    in_bias = noise(key_of[2], (HID,), 0.5, 3.0, (), jnp.float32)
    out_weight = noise(key_of[3], (NVAR, HID), HID ** -0.5, 0.1875)
    out_bias = noise(key_of[4], (NVAR,), 1.0, 3.0, (), jnp.float32)
    observed = noise(part_splits[5], (NVAR, CELLS), 1.0, 6.0, ((1, 32),), jnp.float32)
    patch_of_cell = draw_patch_of_cell(jax.random.fold_in(key_of[7], 71), part)
    return {"latent": latent, "in_weight": in_weight, "in_bias": in_bias, "out_weight": out_weight, "out_bias": out_bias, "observed": observed, "patch_of_cell": patch_of_cell}


epsilon = 1e-06

def reference(latent, in_weight, in_bias, out_weight, out_bias, observed, patch_of_cell):
    in_patch = (patch_of_cell[:, None] == jnp.arange(NPATCH, dtype=jnp.int32)[None, :]).astype(jnp.float32)
    entries = float(NVAR * PATCH)

    def forward(rows):
        preact = jnp.dot(rows, in_weight, preferred_element_type=jnp.float32) + in_bias
        hidden = jax.nn.silu(preact).astype(jnp.bfloat16)
        return (jnp.dot(hidden, out_weight.T, preferred_element_type=jnp.float32).T + out_bias[:, None]).astype(jnp.bfloat16)
    fields = lax.map(forward, latent)
    own_field = fields.astype(jnp.float32)
    misfit = own_field - observed[None]
    obs_sum = jnp.dot(lax.optimization_barrier(jnp.sum(misfit * misfit, axis=1)), in_patch, precision=lax.Precision.HIGHEST)

    def pairs(member):
        diff = member[None] - own_field
        return jnp.dot(lax.optimization_barrier(jnp.sum(diff * diff, axis=1)), in_patch, precision=lax.Precision.HIGHEST)
    pair_sum = lax.map(pairs, own_field)
    spread = jnp.sqrt(obs_sum / entries + epsilon)
    dist = jnp.sqrt(pair_sum / entries + epsilon)
    member_ids = jnp.arange(MEMBERS, dtype=jnp.int32)
    inv_dist = jnp.where((member_ids[:, None] != member_ids[None, :])[:, :, None], 1.0 / dist, jnp.float32(0.0))
    cell_spread = spread[:, patch_of_cell]

    def combine(items):
        inv_row, member = items
        cell_w = inv_row[:, patch_of_cell]
        return lax.optimization_barrier(jnp.sum(cell_w[:, None, :] * (member[None] - own_field), axis=0))
    pulled = lax.map(combine, (inv_dist, own_field))
    grad_field = (misfit / cell_spread[:, None, :] - pulled / MEMBERS).astype(jnp.bfloat16)

    def backward(carry, items):
        rows, grad_one = items
        preact = jnp.dot(rows, in_weight, preferred_element_type=jnp.float32) + in_bias
        hidden = jax.nn.silu(preact).astype(jnp.bfloat16)
        d_hidden = jnp.dot(grad_one.T, out_weight, preferred_element_type=jnp.float32)
        gate_sig = jax.nn.sigmoid(preact)
        d_preact = (d_hidden * gate_sig * (1.0 + preact * (1.0 - gate_sig))).astype(jnp.bfloat16)
        d_rows = jnp.dot(d_preact, in_weight.T, preferred_element_type=jnp.float32).astype(jnp.bfloat16)
        acc_in, acc_out, acc_bin, acc_bout = carry
        acc_in = acc_in + jnp.dot(rows.T, d_preact, preferred_element_type=jnp.float32)
        acc_out = acc_out + jnp.dot(grad_one, hidden, preferred_element_type=jnp.float32)
        acc_bin = acc_bin + lax.optimization_barrier(jnp.sum(d_preact.astype(jnp.float32), axis=0))
        acc_bout = acc_bout + lax.optimization_barrier(jnp.sum(grad_one.astype(jnp.float32), axis=1))
        return ((acc_in, acc_out, acc_bin, acc_bout), d_rows)
    start = (jnp.zeros((D, HID), jnp.float32), jnp.zeros((NVAR, HID), jnp.float32), jnp.zeros((HID,), jnp.float32), jnp.zeros((NVAR,), jnp.float32))
    sums, d_latent = lax.scan(backward, start, (latent, grad_field))
    scale = 1.0 / jnp.sqrt(jnp.float32(MEMBERS * CELLS))
    return (d_latent, sums[0] * scale, sums[1] * scale, sums[2] * scale, sums[3] * scale)
```

```python
import jax
import jax.numpy as jnp
from jax import lax
from jax.sharding import Mesh
from jax.sharding import PartitionSpec as P

epsilon = 1e-06
LAT = ("band", "yl", "x")
GROUP = ("yl", "x")


def gather(block, axes, count):
    return lax.all_to_all(jnp.broadcast_to(block[None], (count, *block.shape)), axes, 0, 0)


def local(latent, in_weight, in_bias, out_weight, out_bias, observed, patch_of_cell):
    members_here, cells_here, width = latent.shape
    hid = in_weight.shape[1]
    n_mem = lax.axis_size("mem")
    n_lat = lax.axis_size(LAT)
    n_group = lax.axis_size(GROUP)
    members = members_here * n_mem
    nvars = out_weight.shape[0]
    entries = float(nvars * 4 * cells_here)
    highest = lax.Precision.HIGHEST
    preact = (
        jnp.einsum("mcd,dk->mck", latent, in_weight, preferred_element_type=jnp.float32) + in_bias
    )
    hidden = jax.nn.silu(preact).astype(jnp.bfloat16)
    field = (
        jnp.einsum("mck,vk->mvc", hidden, out_weight, preferred_element_type=jnp.float32)
        + out_bias[None, :, None]
    ).astype(jnp.bfloat16)
    own_patch = patch_of_cell - 2 * lax.axis_index("band")
    in_patch = (own_patch[:, None] == jnp.arange(2, dtype=jnp.int32)[None, :]).astype(jnp.float32)
    own_field = field.astype(jnp.float32)
    misfit = own_field - observed[None]
    obs_part = jnp.dot(jnp.sum(misfit * misfit, axis=1), in_patch, precision=highest)
    all_fields = gather(field.reshape(members_here * nvars, cells_here), "mem", n_mem)
    all_fields = all_fields.reshape(members, nvars, cells_here)
    diff = own_field[:, None] - all_fields.astype(jnp.float32)[None]
    squared = jnp.sum(diff * diff, axis=2)
    pair_part = jnp.einsum("mnc,cp->mnp", squared, in_patch, precision=highest)
    flat = jnp.concatenate([pair_part.reshape(-1), obs_part.reshape(-1)])
    room = -(-flat.size // 1024) * 1024
    flat = jnp.pad(flat, (0, room - flat.size)).reshape(-1, 128)
    sums = jnp.sum(gather(flat, GROUP, n_group), axis=0).reshape(-1)
    pair_sum = sums[: members_here * members * 2].reshape(members_here, members, 2)
    obs_sum = sums[members_here * members * 2 :][: members_here * 2].reshape(members_here, 2)
    spread = jnp.sqrt(obs_sum / entries + epsilon)
    dist = jnp.sqrt(pair_sum / entries + epsilon)
    own_ids = lax.axis_index("mem") * members_here + jnp.arange(members_here, dtype=jnp.int32)
    other_ids = jnp.arange(members, dtype=jnp.int32)
    inv_dist = jnp.where(
        (own_ids[:, None] != other_ids[None, :])[:, :, None], 1.0 / dist, jnp.float32(0.0)
    )
    first = (own_patch == 0)[None, None, :]
    cell_w = jnp.where(first, inv_dist[:, :, :1], inv_dist[:, :, 1:])
    cell_spread = jnp.where(first[0], spread[:, :1], spread[:, 1:])
    pulled = jnp.sum(cell_w[:, :, None, :] * diff, axis=1)
    grad_field = (misfit / cell_spread[:, None, :] - pulled / members).astype(jnp.bfloat16)
    d_hidden = jnp.einsum("mvc,vk->mck", grad_field, out_weight, preferred_element_type=jnp.float32)
    gate_sig = jax.nn.sigmoid(preact)
    d_preact = (d_hidden * gate_sig * (1.0 + preact * (1.0 - gate_sig))).astype(jnp.bfloat16)
    d_latent = jnp.einsum(
        "mck,dk->mcd", d_preact, in_weight, preferred_element_type=jnp.float32
    ).astype(jnp.bfloat16)
    out_part = jnp.einsum("mvc,mck->vk", grad_field, hidden, preferred_element_type=jnp.float32)
    bin_part = jnp.sum(d_preact, axis=(0, 1), dtype=jnp.float32)
    bout_part = jnp.sum(grad_field, axis=(0, 2), dtype=jnp.float32)
    in_part = jnp.einsum("mcd,mck->dk", latent, d_preact, preferred_element_type=jnp.float32)
    small = jnp.concatenate(
        [out_part.reshape(-1, 128), bin_part.reshape(-1, 128), jnp.pad(bout_part, (0, 128 - nvars))[None]]
    )
    small = jnp.pad(small, ((0, width - small.shape[0]), (0, 0)))
    rows = width // n_lat
    payload = jnp.concatenate([in_part, small], axis=1).reshape(n_lat, rows, hid + 128)
    share = jnp.sum(lax.all_to_all(payload, LAT, 0, 0), axis=0)
    share = jnp.sum(gather(share, "mem", n_mem), axis=0)
    scale = 1.0 / jnp.sqrt(jnp.float32(members * cells_here * n_lat))
    share = share * scale
    high = share.astype(jnp.bfloat16)
    low = (share[:, hid:] - high[:, hid:].astype(jnp.float32)).astype(jnp.bfloat16)
    whole = gather(jnp.concatenate([high, low], axis=1), LAT, n_lat)
    whole = whole.reshape(width, hid + 256).astype(jnp.float32)
    d_in = whole[:, :hid]
    small = whole[:, hid : hid + 128] + whole[:, hid + 128 :]
    n_out = nvars * hid // 128
    n_bin = hid // 128
    d_out = small[:n_out].reshape(nvars, hid)
    d_bin = small[n_out : n_out + n_bin].reshape(hid)
    d_bout = small[n_out + n_bin, :nvars]
    return (d_latent, d_in, d_out, d_bin, d_bout)


def solution(mesh):
    n_mem, n_lat, n_rep = (mesh.shape[a] for a in ("mem", "lat", "rep"))
    split = Mesh(
        mesh.devices.reshape(n_mem, n_lat // 8, 2, 4, n_rep), ("mem", "band", "yl", "x", "rep")
    )
    placed = (P(("rep", "mem"), LAT, None), P(), P(), P(), P(), P("rep", LAT), P(LAT))
    return jax.shard_map(
        local,
        mesh=split,
        in_specs=placed,
        out_specs=(
            P(("rep", "mem"), LAT, None),
            P("rep", None),
            P("rep", None),
            P("rep"),
            P("rep"),
        ),
        check_vma=False,
    )
```

```python
import functools

import jax
import jax.numpy as jnp
from jax import lax
from jax.experimental import pallas as pl
from jax.experimental.pallas import tpu as pltpu
from jax.sharding import Mesh
from jax.sharding import PartitionSpec as P

epsilon = 1e-06
LAT = ("band", "yl", "x")
GROUP = ("yl", "x")
f32, bf16 = jnp.float32, jnp.bfloat16
NN = (((1,), (0,)), ((), ()))
NT = (((1,), (1,)), ((), ()))
TN = (((0,), (0,)), ((), ()))
LANES = 128
TAIL = 8
PARAMS = pltpu.CompilerParams(vmem_limit_bytes=48 * 2**20)


def dot(a, b, dims):
    return lax.dot_general(a, b, dims, preferred_element_type=f32)


def exchange(blocks, axes):
    return lax.all_to_all(blocks, axes, 0, 0)


def quantize(block):
    top = jnp.max(jnp.abs(block), keepdims=True)
    exponent = jnp.clip(jnp.ceil(jnp.log2(jnp.maximum(top, 1e-33))), -110.0, 110.0)
    whole = jnp.clip(jnp.round(block * jnp.exp2(15.0 - exponent)), -32767.0, 32767.0)
    return whole.astype(jnp.int32), exponent.astype(jnp.int32)


def encode(block, tail):
    row = lax.broadcasted_iota(jnp.int32, tail.shape, 0)
    codes, exponent = quantize(block)
    tail_codes, tail_exponent = quantize(jnp.where(row < TAIL - 2, tail, 0.0))
    last = jnp.where(
        row == TAIL - 2, exponent, jnp.where(row == TAIL - 1, tail_exponent, tail_codes)
    )
    return jnp.concatenate([codes, last], axis=0).astype(jnp.int16)


def decode(chunk):
    values = chunk.astype(jnp.int32).astype(f32)
    rows = values.shape[0] - TAIL
    block = values[:rows] * jnp.exp2(values[rows + TAIL - 2 : rows + TAIL - 1] - 15.0)
    tail = values[rows:] * jnp.exp2(values[rows + TAIL - 1 :] - 15.0)
    row = lax.broadcasted_iota(jnp.int32, tail.shape, 0)
    return block, jnp.where(row < TAIL - 2, tail, 0.0)


def forward_kernel(n_blocks, x_ref, w_ref, b_ref, wo_ref, bo_ref, f_ref):
    x = x_ref[0]
    step = w_ref.shape[1] // n_blocks
    total = bo_ref[...]
    for k in range(n_blocks):
        cols = slice(k * step, (k + 1) * step)
        half = 0.5 * (dot(x, w_ref[:, cols], NN) + b_ref[:, cols])
        hidden = (half * jnp.tanh(half) + half).astype(bf16)
        total = total + dot(wo_ref[:, cols], hidden, NT)
    field = total.astype(bf16)
    for copy in range(f_ref.shape[0]):
        f_ref[copy, pl.program_id(0)] = field


def forward(latent, w, b, wo, bo, copies):
    members, cells, width = latent.shape
    nvars, hid = wo.shape
    const = lambda i: (0, 0)
    return pl.pallas_call(
        functools.partial(forward_kernel, 8),
        grid=(members,),
        in_specs=[
            pl.BlockSpec((1, cells, width), lambda i: (i, 0, 0)),
            pl.BlockSpec((width, hid), const),
            pl.BlockSpec((1, hid), const),
            pl.BlockSpec((nvars, hid), const),
            pl.BlockSpec((nvars, 1), const),
        ],
        out_specs=pl.BlockSpec((copies, members, nvars, cells), lambda i: (0, 0, 0, 0)),
        out_shape=jax.ShapeDtypeStruct((copies, members, nvars, cells), bf16),
        compiler_params=PARAMS,
        name="field",
    )(latent, w, b.reshape(1, hid), wo, bo.reshape(nvars, 1))


def backward_kernel(n_blocks, x_ref, w_ref, b_ref, wo_ref, g_ref, dp_ref, pay_ref, acc, small):
    member = pl.program_id(0)

    @pl.when(member == 0)
    def _():
        acc[...] = jnp.zeros_like(acc)
        small[...] = jnp.zeros_like(small)

    x = x_ref[0]
    g = g_ref[0]
    nvars = g.shape[0]
    step = w_ref.shape[1] // n_blocks
    ones = jnp.ones((8, x.shape[0]), bf16)
    for k in range(n_blocks):
        cols = slice(k * step, (k + 1) * step)
        pre = dot(x, w_ref[:, cols], NN) + b_ref[:, cols]
        sig = 0.5 * jnp.tanh(0.5 * pre) + 0.5
        act = pre * sig
        slope = act * (1.0 - sig) + sig
        dp = (dot(g, wo_ref[:, cols], TN) * slope).astype(bf16)
        dp_ref[0, :, cols] = dp
        acc[:, cols] += dot(x, dp, TN)
        small[0:nvars, cols] += dot(g, act.astype(bf16), NN)
        small[nvars : nvars + 1, cols] += dot(ones, dp, NN)[0:1]
    bias = jnp.sum(g.astype(f32), axis=1, keepdims=True)
    for v in range(nvars):
        small[nvars + 1 : nvars + 2, v * LANES : (v + 1) * LANES] += jnp.broadcast_to(
            bias[v : v + 1], (1, LANES)
        )

    @pl.when(member == pl.num_programs(0) - 1)
    def _():
        n_col = acc.shape[1] // LANES
        rows = acc.shape[0] // (pay_ref.shape[0] // n_col)
        owned = [(0, nvars), (nvars, nvars + 1), (nvars + 1, nvars + 2), (0, 0)]
        for rb, (low, high) in enumerate(owned):
            for cb in range(n_col):
                lanes = slice(cb * LANES, (cb + 1) * LANES)
                row = lax.broadcasted_iota(jnp.int32, (TAIL, LANES), 0)
                tail = jnp.where((row >= low) & (row < high), small[:, lanes], 0.0)
                pay_ref[rb * n_col + cb] = encode(acc[rb * rows : (rb + 1) * rows, lanes], tail)


def backward(latent, w, b, wo, g, chunks):
    members, cells, width = latent.shape
    nvars, hid = wo.shape
    const = lambda i: (0, 0)
    chunk = (width * hid // (chunks * LANES) + TAIL, LANES)
    return pl.pallas_call(
        functools.partial(backward_kernel, 8),
        grid=(members,),
        in_specs=[
            pl.BlockSpec((1, cells, width), lambda i: (i, 0, 0)),
            pl.BlockSpec((width, hid), const),
            pl.BlockSpec((1, hid), const),
            pl.BlockSpec((nvars, hid), const),
            pl.BlockSpec((1, nvars, cells), lambda i: (i, 0, 0)),
        ],
        out_specs=[
            pl.BlockSpec((1, cells, hid), lambda i: (i, 0, 0)),
            pl.BlockSpec((chunks, *chunk), lambda i: (0, 0, 0)),
        ],
        out_shape=[
            jax.ShapeDtypeStruct((members, cells, hid), bf16),
            jax.ShapeDtypeStruct((chunks, *chunk), jnp.int16),
        ],
        scratch_shapes=[pltpu.VMEM((width, hid), f32), pltpu.VMEM((TAIL, hid), f32)],
        compiler_params=PARAMS,
        name="backward",
    )(latent, w, b.reshape(1, hid), wo, g)


def down_kernel(dp_ref, w_ref, o_ref):
    o_ref[0] = dot(dp_ref[0], w_ref[...], NT).astype(bf16)


def down(dp, w):
    members, cells, hid = dp.shape
    width = w.shape[0]
    return pl.pallas_call(
        down_kernel,
        grid=(members,),
        in_specs=[
            pl.BlockSpec((1, cells, hid), lambda i: (i, 0, 0)),
            pl.BlockSpec((width, hid), lambda i: (0, 0)),
        ],
        out_specs=pl.BlockSpec((1, cells, width), lambda i: (i, 0, 0)),
        out_shape=jax.ShapeDtypeStruct((members, cells, width), bf16),
        compiler_params=PARAMS,
        name="d_latent",
    )(dp, w)


def reduce_kernel(scale, in_ref, out_ref):
    total, tail = decode(in_ref[0])
    for source in range(1, in_ref.shape[0]):
        block, more = decode(in_ref[source])
        total, tail = total + block, tail + more
    chunk = encode(total * scale, tail * scale)
    for copy in range(out_ref.shape[0]):
        out_ref[copy] = chunk


def reduce_and_copy(received, copies, scale, name):
    return pl.pallas_call(
        functools.partial(reduce_kernel, scale),
        out_shape=jax.ShapeDtypeStruct((copies, *received.shape[1:]), jnp.int16),
        compiler_params=PARAMS,
        name=name,
    )(received)


def spread_kernel(in_ref, d_in_ref, small_ref):
    n_col = d_in_ref.shape[1] // LANES
    rows = in_ref.shape[1] - TAIL
    for cb in range(n_col):
        lanes = slice(cb * LANES, (cb + 1) * LANES)
        tails = None
        for rb in range(in_ref.shape[0] // n_col):
            block, tail = decode(in_ref[rb * n_col + cb])
            d_in_ref[rb * rows : (rb + 1) * rows, lanes] = block
            tails = tail if tails is None else tails + tail
        small_ref[:, lanes] = tails


def spread_out(received, width, hid):
    return pl.pallas_call(
        spread_kernel,
        out_shape=[
            jax.ShapeDtypeStruct((width, hid), f32),
            jax.ShapeDtypeStruct((TAIL, hid), f32),
        ],
        compiler_params=PARAMS,
        name="outputs",
    )(received)


def local(latent, in_weight, in_bias, out_weight, out_bias, observed, patch_of_cell):
    members_here, cells_here, width = latent.shape
    nvars, hid = out_weight.shape
    n_mem = lax.axis_size("mem")
    n_lat = lax.axis_size(LAT)
    n_group = lax.axis_size(GROUP)
    members = members_here * n_mem
    entries = float(nvars * 4 * cells_here)
    highest = lax.Precision.HIGHEST
    copies = forward(latent, in_weight, in_bias, out_weight, out_bias, n_mem)
    all_fields = exchange(copies, "mem").reshape(members, nvars, cells_here).astype(f32)
    own_field = copies[0].astype(f32)
    own_patch = patch_of_cell - 2 * lax.axis_index("band")
    in_patch = (own_patch[:, None] == jnp.arange(2, dtype=jnp.int32)[None, :]).astype(f32)
    misfit = own_field - observed[None]
    obs_part = jnp.dot(jnp.sum(misfit * misfit, axis=1), in_patch, precision=highest)
    diff = own_field[:, None] - all_fields[None]
    squared = jnp.sum(diff * diff, axis=2)
    pair_part = jnp.einsum("mnc,cp->mnp", squared, in_patch, precision=highest)
    flat = jnp.concatenate([pair_part.reshape(-1), obs_part.reshape(-1)])
    room = -(-flat.size // 1024) * 1024
    flat = jnp.pad(flat, (0, room - flat.size)).reshape(-1, 128)
    sums = exchange(jnp.broadcast_to(flat[None], (n_group, *flat.shape)), GROUP)
    sums = jnp.sum(sums, axis=0).reshape(-1)
    pair_sum = sums[: members_here * members * 2].reshape(members_here, members, 2)
    obs_sum = sums[members_here * members * 2 :][: members_here * 2].reshape(members_here, 2)
    spread = jnp.sqrt(obs_sum / entries + epsilon)
    dist = jnp.sqrt(pair_sum / entries + epsilon)
    own_ids = lax.axis_index("mem") * members_here + jnp.arange(members_here, dtype=jnp.int32)
    other_ids = jnp.arange(members, dtype=jnp.int32)
    inv_dist = jnp.where(
        (own_ids[:, None] != other_ids[None, :])[:, :, None], 1.0 / dist, jnp.float32(0.0)
    )
    first = (own_patch == 0)[None, None, :]
    cell_w = jnp.where(first, inv_dist[:, :, :1], inv_dist[:, :, 1:])
    cell_spread = jnp.where(first[0], spread[:, :1], spread[:, 1:])
    pulled = jnp.sum(cell_w[:, :, None, :] * diff, axis=1)
    grad_field = (misfit / cell_spread[:, None, :] - pulled / members).astype(bf16)
    d_preact, payload = backward(latent, in_weight, in_bias, out_weight, grad_field, n_lat)
    d_latent = down(d_preact, in_weight)
    scale = 1.0 / (members * cells_here * n_lat) ** 0.5
    payload = reduce_and_copy(exchange(payload, LAT), n_mem, 1.0, "lat_sum")
    payload = reduce_and_copy(exchange(payload, "mem"), n_lat, scale, "mem_sum")
    d_in, small = spread_out(exchange(payload, LAT), width, hid)
    d_bout = small[nvars + 1].reshape(-1, LANES)[:nvars, 0]
    return (d_latent, d_in, small[:nvars], small[nvars], d_bout)


def solution(mesh):
    n_mem, n_lat, n_rep = (mesh.shape[a] for a in ("mem", "lat", "rep"))
    split = Mesh(
        mesh.devices.reshape(n_mem, n_lat // 8, 2, 4, n_rep), ("mem", "band", "yl", "x", "rep")
    )
    placed = (P(("rep", "mem"), LAT, None), P(), P(), P(), P(), P("rep", LAT), P(LAT))
    return jax.shard_map(
        local,
        mesh=split,
        in_specs=placed,
        out_specs=(
            P(("rep", "mem"), LAT, None),
            P("rep", None),
            P("rep", None),
            P("rep"),
            P("rep"),
        ),
        check_vma=False,
    )
```

```python
import functools

import jax
import jax.numpy as jnp
from jax import lax
from jax.experimental import pallas as pl
from jax.experimental.pallas import tpu as pltpu
from jax.sharding import Mesh
from jax.sharding import PartitionSpec as P

epsilon = 1e-06
LAT = ("band", "yl", "x")
GROUP = ("yl", "x")
f32, bf16 = jnp.float32, jnp.bfloat16
NN = (((1,), (0,)), ((), ()))
NT = (((1,), (1,)), ((), ()))
TN = (((0,), (0,)), ((), ()))
LANES = 128
TAIL = 8
EXTRA = 16
IN_VMEM = pl.BlockSpec(memory_space=pltpu.VMEM)
PARAMS = pltpu.CompilerParams(vmem_limit_bytes=40 * 2**20)


def dot(a, b, dims):
    return lax.dot_general(a, b, dims, preferred_element_type=f32)


def exchange(blocks, axes):
    return lax.all_to_all(blocks, axes, 0, 0)


def quantize(block):
    top = jnp.max(jnp.abs(block), keepdims=True)
    exponent = jnp.clip(jnp.ceil(jnp.log2(jnp.maximum(top, 1e-33))), -110.0, 110.0)
    whole = jnp.clip(jnp.round(block * jnp.exp2(15.0 - exponent)), -32767.0, 32767.0)
    return whole.astype(jnp.int32), exponent.astype(jnp.int32)


def encode(block, tail):
    row = lax.broadcasted_iota(jnp.int32, tail.shape, 0)
    codes, exponent = quantize(block)
    tail_codes, tail_exponent = quantize(jnp.where(row < TAIL - 2, tail, 0.0))
    last = jnp.where(
        row == TAIL - 2, exponent, jnp.where(row == TAIL - 1, tail_exponent, tail_codes)
    )
    return jnp.concatenate([codes, last], axis=0).astype(jnp.int16)


def decode(chunk):
    values = chunk.astype(jnp.int32).astype(f32)
    rows = values.shape[0] - TAIL
    block = values[:rows] * jnp.exp2(values[rows + TAIL - 2 : rows + TAIL - 1] - 15.0)
    tail = values[rows:] * jnp.exp2(values[rows + TAIL - 1 :] - 15.0)
    row = lax.broadcasted_iota(jnp.int32, tail.shape, 0)
    return block, jnp.where(row < TAIL - 2, tail, 0.0)


def blocks(members, hid):
    step = hid // 4
    return [(m, slice(k * step, (k + 1) * step)) for m in range(members) for k in range(4)]


def field_kernel(
    x_hbm, w_hbm, b_hbm, wo_hbm, bo_hbm, f_ref, x_ref, w_ref, b_ref, wo_ref, bo_ref, sems
):
    members = x_ref.shape[0]
    sources = [(w_hbm, w_ref), (x_hbm.at[0], x_ref.at[0]), (b_hbm, b_ref), (wo_hbm, wo_ref)]
    sources.append((bo_hbm, bo_ref))
    sources += [(x_hbm.at[m], x_ref.at[m]) for m in range(1, members)]
    loads = [
        pltpu.make_async_copy(source, target, sems.at[i])
        for i, (source, target) in enumerate(sources)
    ]
    for load in loads:
        load.start()
    for load in loads[:5]:
        load.wait()
    nvars, hid = wo_ref.shape
    square = (nvars, nvars)
    diagonal = lax.broadcasted_iota(jnp.int32, square, 0) == lax.broadcasted_iota(
        jnp.int32, square, 1
    )
    bias = jnp.sum(jnp.where(diagonal, bo_ref[...], 0.0), axis=1, keepdims=True)
    totals = [bias] * members
    waiting = None

    def second_layer(m, cols, hidden):
        totals[m] = totals[m] + dot(wo_ref[:, cols], hidden, NT)

    for m, cols in blocks(members, hid):
        if m > 0 and cols.start == 0:
            loads[4 + m].wait()
        half = 0.5 * (dot(x_ref[m], w_ref[:, cols], NN) + b_ref[:, cols])
        hidden = (half * jnp.tanh(half) + half).astype(bf16)
        if waiting is not None:
            second_layer(*waiting)
        waiting = (m, cols, hidden)
    second_layer(*waiting)
    for m in range(members):
        field = totals[m].astype(bf16)
        for copy in range(f_ref.shape[0]):
            f_ref[copy, m] = field


def forward(latent, w, b, wo, bo, copies):
    pinned = [pltpu.with_memory_space_constraint(a, pltpu.HBM) for a in (latent, w, b.reshape(1, -1), wo, bo.reshape(1, -1))]
    members, cells, _ = latent.shape
    nvars, hid = wo.shape
    in_hbm = pl.BlockSpec(memory_space=pltpu.HBM)
    return pl.pallas_call(
        field_kernel,
        in_specs=[in_hbm] * 5,
        out_shape=[
            jax.ShapeDtypeStruct((copies, members, nvars, cells), bf16),
            pltpu.VMEM(latent.shape, bf16),
            pltpu.VMEM(w.shape, bf16),
            pltpu.VMEM((1, hid), f32),
            pltpu.VMEM(wo.shape, bf16),
        ],
        out_specs=[IN_VMEM] * 5,
        scratch_shapes=[pltpu.VMEM((1, nvars), f32), pltpu.SemaphoreType.DMA((4 + members,))],
        compiler_params=PARAMS,
        name="field",
    )(*pinned)


def member_block(*dims):
    return pl.BlockSpec((1, *dims), lambda i: (i, 0, 0))


def whole(array):
    return pl.BlockSpec(array.shape, lambda i: (0,) * array.ndim)


def backward_kernel(
    x_ref, w_ref, b_ref, wo_ref, g_ref, dp_hbm, pay_ref, dp_ref, acc, small, xt, sems
):
    members, cells, width = x_ref.shape
    nvars, hid = wo_ref.shape
    bias = None
    for m in range(members):
        sums = jnp.sum(g_ref[m].astype(f32), axis=1, keepdims=True)
        bias = sums if bias is None else bias + sums
        xt[m, :width] = x_ref[m].T
        xt[m, width:] = jnp.ones((EXTRA, cells), bf16)

    saves = [
        pltpu.make_async_copy(dp_ref.at[m], dp_hbm.at[m], sems.at[m]) for m in range(members)
    ]

    def add(m, cols, dp, hidden):
        d_in, d_out = dot(xt[m], dp, NN), dot(g_ref[m], hidden, NN)
        if m == 0:
            acc[:, cols], small[:, cols] = d_in, d_out
        else:
            acc[:, cols] += d_in
            small[:, cols] += d_out

    waiting = None
    for m, cols in blocks(members, hid):
        pre = dot(x_ref[m], w_ref[:, cols], NN) + b_ref[:, cols]
        sig = 0.5 * jnp.tanh(0.5 * pre) + 0.5
        act = pre * sig
        slope = act * (1.0 - sig) + sig
        dp = (dot(g_ref[m], wo_ref[:, cols], TN) * slope).astype(bf16)
        dp_ref[m, :, cols] = dp
        if cols.stop == hid:
            saves[m].start()
        if waiting is not None:
            add(*waiting)
        waiting = (m, cols, dp, act.astype(bf16))
    add(*waiting)

    n_col = hid // LANES
    rows = width // (pay_ref.shape[0] // n_col)
    row = lax.broadcasted_iota(jnp.int32, (TAIL, LANES), 0)
    empty = jnp.zeros((TAIL - nvars, LANES), f32)
    for cb in range(n_col):
        lanes = slice(cb * LANES, (cb + 1) * LANES)
        tails = [jnp.concatenate([small[:, lanes], empty], axis=0)]
        tails.append(jnp.where(row == nvars, acc[width : width + 1, lanes], 0.0))
        sums = bias[cb : cb + 1] if cb < nvars else jnp.zeros((1, 1), f32)
        tails.append(jnp.where(row == nvars + 1, sums, 0.0))
        tails.append(jnp.zeros((TAIL, LANES), f32))
        for rb, tail in enumerate(tails):
            pay_ref[rb * n_col + cb] = encode(acc[rb * rows : (rb + 1) * rows, lanes], tail)
    for save in saves:
        save.wait()


def backward(latent, w, b, wo, g, chunks):
    members, cells, width = latent.shape
    nvars, hid = wo.shape
    return pl.pallas_call(
        backward_kernel,
        in_specs=[IN_VMEM] * 5,
        out_shape=[
            pltpu.HBM((members, cells, hid), bf16),
            pltpu.VMEM((chunks, width * hid // (chunks * LANES) + TAIL, LANES), jnp.int16),
        ],
        out_specs=[pl.BlockSpec(memory_space=pltpu.HBM), IN_VMEM],
        scratch_shapes=[
            pltpu.VMEM((members, cells, hid), bf16),
            pltpu.VMEM((width + EXTRA, hid), f32),
            pltpu.VMEM((nvars, hid), f32),
            pltpu.VMEM((members, width + EXTRA, cells), bf16),
            pltpu.SemaphoreType.DMA((members,)),
        ],
        compiler_params=PARAMS,
        name="backward",
    )(latent, w, b, wo, g)


def down_kernel(dp_ref, w_ref, o_ref):
    o_ref[0] = dot(dp_ref[0], w_ref[...], NT).astype(bf16)


def down(dp, w):
    members, cells, hid = dp.shape
    width = w.shape[0]
    return pl.pallas_call(
        down_kernel,
        grid=(members,),
        in_specs=[member_block(cells, hid), whole(w)],
        out_specs=member_block(cells, width),
        out_shape=jax.ShapeDtypeStruct((members, cells, width), bf16),
        compiler_params=PARAMS,
        name="d_latent",
    )(pltpu.with_memory_space_constraint(dp, pltpu.HBM), w)


def reduce_kernel(scale, in_ref, out_ref):
    total, tail = decode(in_ref[0])
    for source in range(1, in_ref.shape[0]):
        block, more = decode(in_ref[source])
        total, tail = total + block, tail + more
    chunk = encode(total * scale, tail * scale)
    for copy in range(out_ref.shape[0]):
        out_ref[copy] = chunk


def reduce_and_copy(received, copies, scale, name):
    return pl.pallas_call(
        functools.partial(reduce_kernel, scale),
        out_shape=jax.ShapeDtypeStruct((copies, *received.shape[1:]), jnp.int16),
        compiler_params=PARAMS,
        name=name,
    )(received)


def spread_kernel(in_ref, d_in_ref, d_out_ref, d_bin_ref, d_bout_ref):
    n_col = d_in_ref.shape[1] // LANES
    nvars = d_out_ref.shape[0]
    rows = in_ref.shape[1] - TAIL
    for cb in range(n_col):
        lanes = slice(cb * LANES, (cb + 1) * LANES)
        tails = None
        for rb in range(in_ref.shape[0] // n_col):
            block, tail = decode(in_ref[rb * n_col + cb])
            d_in_ref[rb * rows : (rb + 1) * rows, lanes] = block
            tails = tail if tails is None else tails + tail
        d_out_ref[:, lanes] = tails[:nvars]
        d_bin_ref[pl.ds(cb * LANES, LANES)] = tails[nvars]
        if cb < nvars:
            d_bout_ref[cb] = tails[nvars + 1, 0]


def spread_out(received, width, hid, nvars):
    return pl.pallas_call(
        spread_kernel,
        out_shape=[
            jax.ShapeDtypeStruct((width, hid), f32),
            jax.ShapeDtypeStruct((nvars, hid), f32),
            jax.ShapeDtypeStruct((hid,), f32),
            jax.ShapeDtypeStruct((nvars,), f32),
        ],
        out_specs=[IN_VMEM] * 3 + [pl.BlockSpec(memory_space=pltpu.SMEM)],
        compiler_params=PARAMS,
        name="outputs",
    )(received)


def local(latent, in_weight, in_bias, out_weight, out_bias, observed, patch_of_cell):
    members_here, cells_here, width = latent.shape
    nvars, hid = out_weight.shape
    n_mem = lax.axis_size("mem")
    n_lat = lax.axis_size(LAT)
    n_group = lax.axis_size(GROUP)
    members = members_here * n_mem
    entries = float(nvars * 4 * cells_here)
    highest = lax.Precision.HIGHEST
    copies, latent, in_weight, in_bias, out_weight = forward(
        latent, in_weight, in_bias, out_weight, out_bias, n_mem
    )
    all_fields = exchange(copies, "mem").reshape(members, nvars, cells_here).astype(f32)
    own_field = copies[0].astype(f32)
    own_patch = patch_of_cell - 2 * lax.axis_index("band")
    in_patch = (own_patch[:, None] == jnp.arange(2, dtype=jnp.int32)[None, :]).astype(f32)
    misfit = own_field - observed[None]
    obs_part = jnp.dot(jnp.sum(misfit * misfit, axis=1), in_patch, precision=highest)
    diff = own_field[:, None] - all_fields[None]
    squared = jnp.sum(diff * diff, axis=2)
    pair_part = jnp.einsum("mnc,cp->mnp", squared, in_patch, precision=highest)
    flat = jnp.concatenate([pair_part.reshape(-1), obs_part.reshape(-1)])
    room = -(-flat.size // 1024) * 1024
    flat = jnp.pad(flat, (0, room - flat.size)).reshape(-1, 128)
    sums = exchange(jnp.broadcast_to(flat[None], (n_group, *flat.shape)), GROUP)
    sums = jnp.sum(sums, axis=0).reshape(-1)
    pair_sum = sums[: members_here * members * 2].reshape(members_here, members, 2)
    obs_sum = sums[members_here * members * 2 :][: members_here * 2].reshape(members_here, 2)
    spread = jnp.sqrt(obs_sum / entries + epsilon)
    dist = jnp.sqrt(pair_sum / entries + epsilon)
    own_ids = lax.axis_index("mem") * members_here + jnp.arange(members_here, dtype=jnp.int32)
    other_ids = jnp.arange(members, dtype=jnp.int32)
    inv_dist = jnp.where(
        (own_ids[:, None] != other_ids[None, :])[:, :, None], 1.0 / dist, jnp.float32(0.0)
    )
    first = (own_patch == 0)[None, None, :]
    cell_w = jnp.where(first, inv_dist[:, :, :1], inv_dist[:, :, 1:])
    cell_spread = jnp.where(first[0], spread[:, :1], spread[:, 1:])
    pulled = jnp.sum(cell_w[:, :, None, :] * diff, axis=1)
    grad_field = (misfit / cell_spread[:, None, :] - pulled / members).astype(bf16)
    d_preact, payload = backward(latent, in_weight, in_bias, out_weight, grad_field, n_lat)
    d_latent = down(d_preact, in_weight)
    scale = 1.0 / (members * cells_here * n_lat) ** 0.5
    payload = reduce_and_copy(exchange(payload, LAT), n_mem, 1.0, "lat_sum")
    payload = reduce_and_copy(exchange(payload, "mem"), n_lat, scale, "mem_sum")
    return (d_latent, *spread_out(exchange(payload, LAT), width, hid, nvars))


def solution(mesh):
    n_mem, n_lat, n_rep = (mesh.shape[a] for a in ("mem", "lat", "rep"))
    split = Mesh(
        mesh.devices.reshape(n_mem, n_lat // 8, 2, 4, n_rep), ("mem", "band", "yl", "x", "rep")
    )
    placed = (P(("rep", "mem"), LAT, None), P(), P(), P(), P(), P("rep", LAT), P(LAT))
    return jax.shard_map(
        local,
        mesh=split,
        in_specs=placed,
        out_specs=(
            P(("rep", "mem"), LAT, None),
            P("rep", None),
            P("rep", None),
            P("rep"),
            P("rep"),
        ),
        check_vma=False,
    )
```

```python
import functools

import jax
import jax.numpy as jnp
from jax import lax
from jax.experimental import pallas as pl
from jax.experimental.pallas import tpu as pltpu
from jax.sharding import Mesh
from jax.sharding import PartitionSpec as P

epsilon = 1e-06
LAT = ("band", "yl", "x")
GROUP = ("yl", "x")
f32, bf16 = jnp.float32, jnp.bfloat16
NN = (((1,), (0,)), ((), ()))
NT = (((1,), (1,)), ((), ()))
TN = (((0,), (0,)), ((), ()))
LANES = 128
TAIL = 8
EXTRA = 16
IN_VMEM = pl.BlockSpec(memory_space=pltpu.VMEM)
PARAMS = pltpu.CompilerParams(vmem_limit_bytes=40 * 2**20)


def dot(a, b, dims):
    return lax.dot_general(a, b, dims, preferred_element_type=f32)


def exchange(blocks, axes):
    return lax.all_to_all(blocks, axes, 0, 0)


def quantize(block):
    top = jnp.max(jnp.abs(block), keepdims=True)
    exponent = jnp.clip(jnp.ceil(jnp.log2(jnp.maximum(top, 1e-33))), -110.0, 110.0)
    whole = jnp.clip(jnp.round(block * jnp.exp2(15.0 - exponent)), -32767.0, 32767.0)
    return whole.astype(jnp.int32), exponent.astype(jnp.int32)


def encode(block, tail):
    row = lax.broadcasted_iota(jnp.int32, tail.shape, 0)
    codes, exponent = quantize(block)
    tail_codes, tail_exponent = quantize(jnp.where(row < TAIL - 2, tail, 0.0))
    last = jnp.where(
        row == TAIL - 2, exponent, jnp.where(row == TAIL - 1, tail_exponent, tail_codes)
    )
    return jnp.concatenate([codes, last], axis=0).astype(jnp.int16)


def decode(chunk):
    values = chunk.astype(jnp.int32).astype(f32)
    rows = values.shape[0] - TAIL
    block = values[:rows] * jnp.exp2(values[rows + TAIL - 2 : rows + TAIL - 1] - 15.0)
    tail = values[rows:] * jnp.exp2(values[rows + TAIL - 1 :] - 15.0)
    row = lax.broadcasted_iota(jnp.int32, tail.shape, 0)
    return block, jnp.where(row < TAIL - 2, tail, 0.0)


def blocks(members, hid):
    step = hid // 4
    return [(m, slice(k * step, (k + 1) * step)) for m in range(members) for k in range(4)]


def field_kernel(
    x_hbm, w_hbm, b_hbm, wo_hbm, bo_hbm, f_ref, x_ref, w_ref, b_ref, wo_ref, bo_ref, sems
):
    members = x_ref.shape[0]
    sources = [(w_hbm, w_ref), (x_hbm.at[0], x_ref.at[0]), (b_hbm, b_ref), (wo_hbm, wo_ref)]
    sources.append((bo_hbm, bo_ref))
    sources += [(x_hbm.at[m], x_ref.at[m]) for m in range(1, members)]
    loads = [
        pltpu.make_async_copy(source, target, sems.at[i])
        for i, (source, target) in enumerate(sources)
    ]
    for load in loads:
        load.start()
    for load in loads[:5]:
        load.wait()
    nvars, hid = wo_ref.shape
    square = (nvars, nvars)
    diagonal = lax.broadcasted_iota(jnp.int32, square, 0) == lax.broadcasted_iota(
        jnp.int32, square, 1
    )
    bias = jnp.sum(jnp.where(diagonal, bo_ref[...], 0.0), axis=1, keepdims=True)
    totals = [bias] * members
    waiting = None

    def second_layer(m, cols, hidden):
        totals[m] = totals[m] + dot(wo_ref[:, cols], hidden, NT)

    for m, cols in blocks(members, hid):
        if m > 0 and cols.start == 0:
            loads[4 + m].wait()
        half = 0.5 * (dot(x_ref[m], w_ref[:, cols], NN) + b_ref[:, cols])
        hidden = (half * jnp.tanh(half) + half).astype(bf16)
        if waiting is not None:
            second_layer(*waiting)
        waiting = (m, cols, hidden)
    second_layer(*waiting)
    for m in range(members):
        field = totals[m].astype(bf16)
        for copy in range(f_ref.shape[0]):
            f_ref[copy, m] = field


def forward(latent, w, b, wo, bo, copies):
    pinned = [pltpu.with_memory_space_constraint(a, pltpu.HBM) for a in (latent, w, b.reshape(1, -1), wo, bo.reshape(1, -1))]
    members, cells, _ = latent.shape
    nvars, hid = wo.shape
    in_hbm = pl.BlockSpec(memory_space=pltpu.HBM)
    return pl.pallas_call(
        field_kernel,
        in_specs=[in_hbm] * 5,
        out_shape=[
            jax.ShapeDtypeStruct((copies, members, nvars, cells), bf16),
            pltpu.VMEM(latent.shape, bf16),
            pltpu.VMEM(w.shape, bf16),
            pltpu.VMEM((1, hid), f32),
            pltpu.VMEM(wo.shape, bf16),
        ],
        out_specs=[IN_VMEM] * 5,
        scratch_shapes=[pltpu.VMEM((1, nvars), f32), pltpu.SemaphoreType.DMA((4 + members,))],
        compiler_params=PARAMS,
        name="field",
    )(*pinned)


def member_block(*dims):
    return pl.BlockSpec((1, *dims), lambda i: (i, 0, 0))


def whole(array):
    return pl.BlockSpec(array.shape, lambda i: (0,) * array.ndim)


def gradients(entries, n_members, sums_ref, keep_ref, own_ref, misfit_ref, rhs_ref):
    nvars = own_ref.shape[0]
    total = sums_ref[0]
    for source in range(1, sums_ref.shape[0]):
        total = total + sums_ref[source]
    weights = keep_ref[...] / jnp.sqrt(total / entries + epsilon)
    high = weights.astype(bf16).astype(f32)
    middle = (weights - high).astype(bf16).astype(f32)
    pieces = [high, middle, weights - high - middle, jnp.zeros_like(high)]
    pieces = jnp.concatenate(pieces, axis=0).astype(bf16)
    rows = weights.shape[0]

    def per_cell(i):
        out = dot(pieces, rhs_ref[i], NN)
        return out[:rows] + out[rows : 2 * rows] + out[2 * rows : 3 * rows]

    row_total, over_spread = per_cell(nvars), per_cell(nvars + 1)
    parts = []
    for v in range(nvars):
        pulled = own_ref[v] * row_total - per_cell(v)
        parts.append(misfit_ref[v] * over_spread - pulled / n_members)
    return [
        jnp.concatenate([part[m : m + 1] for part in parts], axis=0).astype(bf16)
        for m in range(rows)
    ]


def backward_kernel(
    entries, n_members, x_ref, w_ref, b_ref, wo_ref, sums_ref, keep_ref, own_ref, misfit_ref, rhs_ref,
    dp_hbm, pay_ref, dp_ref, acc, small, xt, sems,
):
    members, cells, width = x_ref.shape
    nvars, hid = wo_ref.shape
    grads = gradients(entries, n_members, sums_ref, keep_ref, own_ref, misfit_ref, rhs_ref)
    bias = None
    for m in range(members):
        sums = jnp.sum(grads[m].astype(f32), axis=1, keepdims=True)
        bias = sums if bias is None else bias + sums
        xt[m, :width] = x_ref[m].T
        xt[m, width:] = jnp.ones((EXTRA, cells), bf16)
    saves = [
        pltpu.make_async_copy(dp_ref.at[m], dp_hbm.at[m], sems.at[m]) for m in range(members)
    ]

    def add(m, cols, dp, hidden):
        d_in, d_out = dot(xt[m], dp, NN), dot(grads[m], hidden, NN)
        if m == 0:
            acc[:, cols], small[:, cols] = d_in, d_out
        else:
            acc[:, cols] += d_in
            small[:, cols] += d_out

    waiting = None
    for m, cols in blocks(members, hid):
        pre = dot(x_ref[m], w_ref[:, cols], NN) + b_ref[:, cols]
        sig = 0.5 * jnp.tanh(0.5 * pre) + 0.5
        act = pre * sig
        slope = act * (1.0 - sig) + sig
        dp = (dot(grads[m], wo_ref[:, cols], TN) * slope).astype(bf16)
        dp_ref[m, :, cols] = dp
        if cols.stop == hid:
            saves[m].start()
        if waiting is not None:
            add(*waiting)
        waiting = (m, cols, dp, act.astype(bf16))
    add(*waiting)

    n_col = hid // LANES
    rows = width // (pay_ref.shape[0] // n_col)
    row = lax.broadcasted_iota(jnp.int32, (TAIL, LANES), 0)
    empty = jnp.zeros((TAIL - nvars, LANES), f32)
    for cb in range(n_col):
        lanes = slice(cb * LANES, (cb + 1) * LANES)
        tails = [jnp.concatenate([small[:, lanes], empty], axis=0)]
        tails.append(jnp.where(row == nvars, acc[width : width + 1, lanes], 0.0))
        sums = bias[cb : cb + 1] if cb < nvars else jnp.zeros((1, 1), f32)
        tails.append(jnp.where(row == nvars + 1, sums, 0.0))
        tails.append(jnp.zeros((TAIL, LANES), f32))
        for rb, tail in enumerate(tails):
            pay_ref[rb * n_col + cb] = encode(acc[rb * rows : (rb + 1) * rows, lanes], tail)
    for save in saves:
        save.wait()


def backward(latent, w, b, wo, field_operands, entries, n_members, chunks):
    members, cells, width = latent.shape
    nvars, hid = wo.shape
    return pl.pallas_call(
        functools.partial(backward_kernel, entries, n_members),
        in_specs=[IN_VMEM] * (4 + len(field_operands)),
        out_shape=[
            pltpu.HBM((members, cells, hid), bf16),
            pltpu.VMEM((chunks, width * hid // (chunks * LANES) + TAIL, LANES), jnp.int16),
        ],
        out_specs=[pl.BlockSpec(memory_space=pltpu.HBM), IN_VMEM],
        scratch_shapes=[
            pltpu.VMEM((members, cells, hid), bf16),
            pltpu.VMEM((width + EXTRA, hid), f32),
            pltpu.VMEM((nvars, hid), f32),
            pltpu.VMEM((members, width + EXTRA, cells), bf16),
            pltpu.SemaphoreType.DMA((members,)),
        ],
        compiler_params=PARAMS,
        name="backward",
    )(latent, w, b, wo, *field_operands)


def down_kernel(dp_ref, w_ref, o_ref):
    o_ref[0] = dot(dp_ref[0], w_ref[...], NT).astype(bf16)


def down(dp, w):
    members, cells, hid = dp.shape
    width = w.shape[0]
    return pl.pallas_call(
        down_kernel,
        grid=(members,),
        in_specs=[member_block(cells, hid), whole(w)],
        out_specs=member_block(cells, width),
        out_shape=jax.ShapeDtypeStruct((members, cells, width), bf16),
        compiler_params=PARAMS,
        name="d_latent",
    )(pltpu.with_memory_space_constraint(dp, pltpu.HBM), w)


def reduce_kernel(scale, in_ref, out_ref):
    total, tail = decode(in_ref[0])
    for source in range(1, in_ref.shape[0]):
        block, more = decode(in_ref[source])
        total, tail = total + block, tail + more
    chunk = encode(total * scale, tail * scale)
    for copy in range(out_ref.shape[0]):
        out_ref[copy] = chunk


def reduce_and_copy(received, copies, scale, name):
    return pl.pallas_call(
        functools.partial(reduce_kernel, scale),
        out_shape=jax.ShapeDtypeStruct((copies, *received.shape[1:]), jnp.int16),
        compiler_params=PARAMS,
        name=name,
    )(received)


def spread_kernel(in_ref, d_in_ref, d_out_ref, d_bin_ref, d_bout_ref):
    n_col = d_in_ref.shape[1] // LANES
    nvars = d_out_ref.shape[0]
    rows = in_ref.shape[1] - TAIL
    for cb in range(n_col):
        lanes = slice(cb * LANES, (cb + 1) * LANES)
        tails = None
        for rb in range(in_ref.shape[0] // n_col):
            block, tail = decode(in_ref[rb * n_col + cb])
            d_in_ref[rb * rows : (rb + 1) * rows, lanes] = block
            tails = tail if tails is None else tails + tail
        d_out_ref[:, lanes] = tails[:nvars]
        d_bin_ref[pl.ds(cb * LANES, LANES)] = tails[nvars]
        if cb < nvars:
            d_bout_ref[cb] = tails[nvars + 1, 0]


def spread_out(received, width, hid, nvars):
    return pl.pallas_call(
        spread_kernel,
        out_shape=[
            jax.ShapeDtypeStruct((width, hid), f32),
            jax.ShapeDtypeStruct((nvars, hid), f32),
            jax.ShapeDtypeStruct((hid,), f32),
            jax.ShapeDtypeStruct((nvars,), f32),
        ],
        out_specs=[IN_VMEM] * 3 + [pl.BlockSpec(memory_space=pltpu.SMEM)],
        compiler_params=PARAMS,
        name="outputs",
    )(received)


def local(latent, in_weight, in_bias, out_weight, out_bias, observed, patch_of_cell):
    members_here, cells_here, width = latent.shape
    nvars, hid = out_weight.shape
    n_mem = lax.axis_size("mem")
    n_lat = lax.axis_size(LAT)
    n_group = lax.axis_size(GROUP)
    members = members_here * n_mem
    entries = float(nvars * 4 * cells_here)
    highest = lax.Precision.HIGHEST
    copies, latent, in_weight, in_bias, out_weight = forward(
        latent, in_weight, in_bias, out_weight, out_bias, n_mem
    )
    all_fields = exchange(copies, "mem").reshape(members, nvars, cells_here).astype(f32)
    own_field = copies[0].astype(f32)
    own_patch = patch_of_cell - 2 * lax.axis_index("band")
    in_patch = (own_patch[:, None] == jnp.arange(2, dtype=jnp.int32)[None, :]).astype(f32)
    misfit = own_field - observed[None]
    obs_part = jnp.dot(jnp.sum(misfit * misfit, axis=1), in_patch, precision=highest)
    diff = own_field[:, None] - all_fields[None]
    squared = jnp.sum(diff * diff, axis=2)
    pair_part = jnp.einsum("mnc,cp->mpn", squared, in_patch, precision=highest)
    flat = jnp.concatenate([pair_part.reshape(members_here, 2 * members), obs_part], axis=1)
    used = 2 * members + 2
    flat = jnp.pad(flat, ((0, TAIL - members_here), (0, LANES - used)))
    sums = exchange(jnp.broadcast_to(flat[None], (n_group, *flat.shape)), GROUP)
    masks = in_patch.T
    by_var = all_fields.transpose(1, 0, 2)
    pairs = (by_var[:, None] * masks[None, :, None]).reshape(nvars, 2 * members, cells_here)
    ones = jnp.broadcast_to(masks[:, None], (2, members, cells_here))
    ones = ones.reshape(1, 2 * members, cells_here)
    upper = jnp.concatenate([pairs, ones, jnp.zeros_like(ones)], axis=0)
    lower = jnp.zeros((nvars + 2, 2, cells_here), f32).at[nvars + 1].set(masks)
    rhs = jnp.concatenate([upper, lower], axis=1)
    rhs = jnp.pad(rhs, ((0, 0), (0, LANES - used), (0, 0))).astype(bf16)
    row = lax.broadcasted_iota(jnp.int32, (TAIL, LANES), 0)
    lane = lax.broadcasted_iota(jnp.int32, (TAIL, LANES), 1)
    own_id = lax.axis_index("mem") * members_here + row
    another = (lane < 2 * members) & (lane % members != own_id)
    wanted = another | ((lane >= 2 * members) & (lane < used))
    keep = (wanted & (row < members_here)).astype(f32)
    fill = ((0, 0), (0, TAIL - members_here), (0, 0))
    own = jnp.pad(own_field.transpose(1, 0, 2), fill)
    off = jnp.pad(misfit.transpose(1, 0, 2), fill)
    d_preact, payload = backward(
        latent,
        in_weight,
        in_bias,
        out_weight,
        (sums, keep, own, off, rhs),
        entries,
        members,
        n_lat,
    )
    d_latent = down(d_preact, in_weight)
    scale = 1.0 / (members * cells_here * n_lat) ** 0.5
    payload = reduce_and_copy(exchange(payload, LAT), n_mem, 1.0, "lat_sum")
    payload = reduce_and_copy(exchange(payload, "mem"), n_lat, scale, "mem_sum")
    return (d_latent, *spread_out(exchange(payload, LAT), width, hid, nvars))


def solution(mesh):
    n_mem, n_lat, n_rep = (mesh.shape[a] for a in ("mem", "lat", "rep"))
    split = Mesh(
        mesh.devices.reshape(n_mem, n_lat // 8, 2, 4, n_rep), ("mem", "band", "yl", "x", "rep")
    )
    placed = (P(("rep", "mem"), LAT, None), P(), P(), P(), P(), P("rep", LAT), P(LAT))
    return jax.shard_map(
        local,
        mesh=split,
        in_specs=placed,
        out_specs=(
            P(("rep", "mem"), LAT, None),
            P("rep", None),
            P("rep", None),
            P("rep"),
            P("rep"),
        ),
        check_vma=False,
    )
```

```python
import functools

import jax
import jax.numpy as jnp
from jax import lax
from jax.experimental import pallas as pl
from jax.experimental.pallas import tpu as pltpu
from jax.sharding import Mesh
from jax.sharding import PartitionSpec as P

epsilon = 1e-06
LAT = ("band", "yl", "x")
GROUP = ("yl", "x")
f32, bf16 = jnp.float32, jnp.bfloat16
NN = (((1,), (0,)), ((), ()))
NT = (((1,), (1,)), ((), ()))
TN = (((0,), (0,)), ((), ()))
LANES = 128
TAIL = 8
EXTRA = 16
IN_VMEM = pl.BlockSpec(memory_space=pltpu.VMEM)
PARAMS = pltpu.CompilerParams(vmem_limit_bytes=40 * 2**20)


def dot(a, b, dims):
    return lax.dot_general(a, b, dims, preferred_element_type=f32)


def exchange(blocks, axes):
    return lax.all_to_all(blocks, axes, 0, 0)


def quantize(block):
    top = jnp.max(jnp.abs(block), keepdims=True)
    exponent = jnp.clip(jnp.ceil(jnp.log2(jnp.maximum(top, 1e-33))), -110.0, 110.0)
    whole = jnp.clip(jnp.round(block * jnp.exp2(15.0 - exponent)), -32767.0, 32767.0)
    return whole.astype(jnp.int32), exponent.astype(jnp.int32)


def encode(block, tail):
    row = lax.broadcasted_iota(jnp.int32, tail.shape, 0)
    codes, exponent = quantize(block)
    tail_codes, tail_exponent = quantize(jnp.where(row < TAIL - 2, tail, 0.0))
    last = jnp.where(
        row == TAIL - 2, exponent, jnp.where(row == TAIL - 1, tail_exponent, tail_codes)
    )
    return jnp.concatenate([codes, last], axis=0).astype(jnp.int16)


def decode(chunk):
    values = chunk.astype(jnp.int32).astype(f32)
    rows = values.shape[0] - TAIL
    block = values[:rows] * jnp.exp2(values[rows + TAIL - 2 : rows + TAIL - 1] - 15.0)
    tail = values[rows:] * jnp.exp2(values[rows + TAIL - 1 :] - 15.0)
    row = lax.broadcasted_iota(jnp.int32, tail.shape, 0)
    return block, jnp.where(row < TAIL - 2, tail, 0.0)


def blocks(members, hid):
    step = hid // 4
    return [(m, slice(k * step, (k + 1) * step)) for m in range(members) for k in range(4)]


def field_kernel(
    x_hbm, w_hbm, b_hbm, wo_hbm, bo_hbm, f_ref, x_ref, w_ref, b_ref, wo_ref, bo_ref, sems
):
    members = x_ref.shape[0]
    sources = [(w_hbm, w_ref), (x_hbm.at[0], x_ref.at[0]), (b_hbm, b_ref), (wo_hbm, wo_ref)]
    sources.append((bo_hbm, bo_ref))
    sources += [(x_hbm.at[m], x_ref.at[m]) for m in range(1, members)]
    loads = [
        pltpu.make_async_copy(source, target, sems.at[i])
        for i, (source, target) in enumerate(sources)
    ]
    for load in loads:
        load.start()
    for load in loads[:5]:
        load.wait()
    nvars, hid = wo_ref.shape
    square = (nvars, nvars)
    diagonal = lax.broadcasted_iota(jnp.int32, square, 0) == lax.broadcasted_iota(
        jnp.int32, square, 1
    )
    bias = jnp.sum(jnp.where(diagonal, bo_ref[...], 0.0), axis=1, keepdims=True)
    totals = [bias] * members
    waiting = None

    def second_layer(m, cols, hidden):
        totals[m] = totals[m] + dot(wo_ref[:, cols], hidden, NT)

    for m, cols in blocks(members, hid):
        if m > 0 and cols.start == 0:
            loads[4 + m].wait()
        half = 0.5 * (dot(x_ref[m], w_ref[:, cols], NN) + b_ref[:, cols])
        hidden = (half * jnp.tanh(half) + half).astype(bf16)
        if waiting is not None:
            second_layer(*waiting)
        waiting = (m, cols, hidden)
    second_layer(*waiting)
    for m in range(members):
        field = totals[m].astype(bf16)
        for copy in range(f_ref.shape[0]):
            f_ref[copy, m] = field


def forward(latent, w, b, wo, bo, copies):
    pinned = [pltpu.with_memory_space_constraint(a, pltpu.HBM) for a in (latent, w, b.reshape(1, -1), wo, bo.reshape(1, -1))]
    members, cells, _ = latent.shape
    nvars, hid = wo.shape
    in_hbm = pl.BlockSpec(memory_space=pltpu.HBM)
    return pl.pallas_call(
        field_kernel,
        in_specs=[in_hbm] * 5,
        out_shape=[
            jax.ShapeDtypeStruct((copies, members, nvars, cells), bf16),
            pltpu.VMEM(latent.shape, bf16),
            pltpu.VMEM(w.shape, bf16),
            pltpu.VMEM((1, hid), f32),
            pltpu.VMEM(wo.shape, bf16),
        ],
        out_specs=[IN_VMEM] * 5,
        scratch_shapes=[pltpu.VMEM((1, nvars), f32), pltpu.SemaphoreType.DMA((4 + members,))],
        compiler_params=PARAMS,
        name="field",
    )(*pinned)


def member_block(*dims):
    return pl.BlockSpec((1, *dims), lambda i: (i, 0, 0))


def whole(array):
    return pl.BlockSpec(array.shape, lambda i: (0,) * array.ndim)


def gradients(entries, n_members, sums_ref, keep_ref, own_ref, misfit_ref, rhs_ref):
    nvars = own_ref.shape[0]
    total = sums_ref[0]
    for source in range(1, sums_ref.shape[0]):
        total = total + sums_ref[source]
    weights = keep_ref[...] / jnp.sqrt(total / entries + epsilon)
    high = weights.astype(bf16).astype(f32)
    middle = (weights - high).astype(bf16).astype(f32)
    pieces = [high, middle, weights - high - middle, jnp.zeros_like(high)]
    pieces = jnp.concatenate(pieces, axis=0).astype(bf16)
    rows = weights.shape[0]

    def per_cell(i):
        out = dot(pieces, rhs_ref[i], NN)
        return out[:rows] + out[rows : 2 * rows] + out[2 * rows : 3 * rows]

    row_total, over_spread = per_cell(nvars), per_cell(nvars + 1)
    parts = []
    for v in range(nvars):
        pulled = own_ref[v] * row_total - per_cell(v)
        parts.append(misfit_ref[v] * over_spread - pulled / n_members)
    return [
        jnp.concatenate([part[m : m + 1] for part in parts], axis=0).astype(bf16)
        for m in range(rows)
    ]


def backward_kernel(
    entries, n_members, x_ref, w_ref, b_ref, wo_ref, sums_ref, keep_ref, own_ref, misfit_ref, rhs_ref,
    dp_hbm, pay_ref, dp_ref, acc, small, xt, sems,
):
    members, cells, width = x_ref.shape
    nvars, hid = wo_ref.shape
    grads = gradients(entries, n_members, sums_ref, keep_ref, own_ref, misfit_ref, rhs_ref)
    bias = None
    for m in range(members):
        sums = jnp.sum(grads[m].astype(f32), axis=1, keepdims=True)
        bias = sums if bias is None else bias + sums
        xt[m, :width] = x_ref[m].T
        xt[m, width:] = jnp.ones((EXTRA, cells), bf16)
    saves = [
        pltpu.make_async_copy(dp_ref.at[m], dp_hbm.at[m], sems.at[m]) for m in range(members)
    ]

    def add(m, cols, dp, hidden):
        d_in, d_out = dot(xt[m], dp, NN), dot(grads[m], hidden, NN)
        if m == 0:
            acc[:, cols], small[:, cols] = d_in, d_out
        else:
            acc[:, cols] += d_in
            small[:, cols] += d_out

    waiting = None
    for m, cols in blocks(members, hid):
        pre = dot(x_ref[m], w_ref[:, cols], NN) + b_ref[:, cols]
        sig = 0.5 * jnp.tanh(0.5 * pre) + 0.5
        act = pre * sig
        slope = act * (1.0 - sig) + sig
        dp = (dot(grads[m], wo_ref[:, cols], TN) * slope).astype(bf16)
        dp_ref[m, :, cols] = dp
        if cols.stop == hid:
            saves[m].start()
        if waiting is not None:
            add(*waiting)
        waiting = (m, cols, dp, act.astype(bf16))
    add(*waiting)

    n_col = hid // LANES
    rows = width // (pay_ref.shape[0] // n_col)
    row = lax.broadcasted_iota(jnp.int32, (TAIL, LANES), 0)
    empty = jnp.zeros((TAIL - nvars, LANES), f32)
    for cb in range(n_col):
        lanes = slice(cb * LANES, (cb + 1) * LANES)
        tails = [jnp.concatenate([small[:, lanes], empty], axis=0)]
        tails.append(jnp.where(row == nvars, acc[width : width + 1, lanes], 0.0))
        sums = bias[cb : cb + 1] if cb < nvars else jnp.zeros((1, 1), f32)
        tails.append(jnp.where(row == nvars + 1, sums, 0.0))
        tails.append(jnp.zeros((TAIL, LANES), f32))
        for rb, tail in enumerate(tails):
            pay_ref[rb * n_col + cb] = encode(acc[rb * rows : (rb + 1) * rows, lanes], tail)
    for save in saves:
        save.wait()


def backward(latent, w, b, wo, field_operands, entries, n_members, chunks):
    members, cells, width = latent.shape
    nvars, hid = wo.shape
    return pl.pallas_call(
        functools.partial(backward_kernel, entries, n_members),
        in_specs=[IN_VMEM] * (4 + len(field_operands)),
        out_shape=[
            pltpu.HBM((members, cells, hid), bf16),
            pltpu.VMEM((chunks, width * hid // (chunks * LANES) + TAIL, LANES), jnp.int16),
        ],
        out_specs=[pl.BlockSpec(memory_space=pltpu.HBM), IN_VMEM],
        scratch_shapes=[
            pltpu.VMEM((members, cells, hid), bf16),
            pltpu.VMEM((width + EXTRA, hid), f32),
            pltpu.VMEM((nvars, hid), f32),
            pltpu.VMEM((members, width + EXTRA, cells), bf16),
            pltpu.SemaphoreType.DMA((members,)),
        ],
        compiler_params=PARAMS,
        name="backward",
    )(latent, w, b, wo, *field_operands)


def down_kernel(dp_ref, w_ref, o_ref):
    o_ref[0] = dot(dp_ref[0], w_ref[...], NT).astype(bf16)


def down(dp, w):
    members, cells, hid = dp.shape
    width = w.shape[0]
    return pl.pallas_call(
        down_kernel,
        grid=(members,),
        in_specs=[member_block(cells, hid), whole(w)],
        out_specs=member_block(cells, width),
        out_shape=jax.ShapeDtypeStruct((members, cells, width), bf16),
        compiler_params=PARAMS,
        name="d_latent",
    )(pltpu.with_memory_space_constraint(dp, pltpu.HBM), w)


def reduce_kernel(scale, in_ref, out_ref):
    total, tail = decode(in_ref[0])
    for source in range(1, in_ref.shape[0]):
        block, more = decode(in_ref[source])
        total, tail = total + block, tail + more
    chunk = encode(total * scale, tail * scale)
    for copy in range(out_ref.shape[0]):
        out_ref[copy] = chunk


def reduce_and_copy(received, copies, scale, name):
    return pl.pallas_call(
        functools.partial(reduce_kernel, scale),
        out_shape=jax.ShapeDtypeStruct((copies, *received.shape[1:]), jnp.int16),
        compiler_params=PARAMS,
        name=name,
    )(received)


def spread_kernel(in_ref, d_in_ref, d_out_ref, d_bin_ref, d_bout_ref):
    n_col = d_in_ref.shape[1] // LANES
    nvars = d_out_ref.shape[0]
    rows = in_ref.shape[1] - TAIL
    for cb in range(n_col):
        lanes = slice(cb * LANES, (cb + 1) * LANES)
        tails = None
        for rb in range(in_ref.shape[0] // n_col):
            block, tail = decode(in_ref[rb * n_col + cb])
            d_in_ref[rb * rows : (rb + 1) * rows, lanes] = block
            tails = tail if tails is None else tails + tail
        d_out_ref[:, lanes] = tails[:nvars]
        d_bin_ref[pl.ds(cb * LANES, LANES)] = tails[nvars]
        if cb < nvars:
            d_bout_ref[cb] = tails[nvars + 1, 0]


def spread_out(received, width, hid, nvars):
    return pl.pallas_call(
        spread_kernel,
        out_shape=[
            jax.ShapeDtypeStruct((width, hid), f32),
            jax.ShapeDtypeStruct((nvars, hid), f32),
            jax.ShapeDtypeStruct((hid,), f32),
            jax.ShapeDtypeStruct((nvars,), f32),
        ],
        out_specs=[IN_VMEM] * 3 + [pl.BlockSpec(memory_space=pltpu.SMEM)],
        compiler_params=PARAMS,
        name="outputs",
    )(received)


def local(latent, in_weight, in_bias, out_weight, out_bias, observed, patch_of_cell):
    members_here, cells_here, width = latent.shape
    nvars, hid = out_weight.shape
    n_mem = lax.axis_size("mem")
    n_lat = lax.axis_size(LAT)
    n_group = lax.axis_size(GROUP)
    members = members_here * n_mem
    entries = float(nvars * 4 * cells_here)
    highest = lax.Precision.HIGHEST
    copies, latent, in_weight, in_bias, out_weight = forward(
        latent, in_weight, in_bias, out_weight, out_bias, n_mem
    )
    all_fields = exchange(copies, "mem").reshape(members, nvars, cells_here).astype(f32)
    own_field = copies[0].astype(f32)
    own_patch = patch_of_cell - 2 * lax.axis_index("band")
    in_patch = (own_patch[:, None] == jnp.arange(2, dtype=jnp.int32)[None, :]).astype(f32)
    misfit = own_field - observed[None]
    obs_part = jnp.dot(jnp.sum(misfit * misfit, axis=1), in_patch, precision=highest)
    diff = own_field[:, None] - all_fields[None]
    squared = jnp.sum(diff * diff, axis=2)
    pair_part = jnp.einsum("mnc,cp->mpn", squared, in_patch, precision=highest)
    flat = jnp.concatenate([pair_part.reshape(members_here, 2 * members), obs_part], axis=1)
    used = 2 * members + 2
    flat = jnp.pad(flat, ((0, TAIL - members_here), (0, LANES - used)))
    sums = exchange(jnp.broadcast_to(flat[None], (n_group, *flat.shape)), GROUP)
    masks = in_patch.T
    by_var = all_fields.transpose(1, 0, 2)
    pairs = (by_var[:, None] * masks[None, :, None]).reshape(nvars, 2 * members, cells_here)
    ones = jnp.broadcast_to(masks[:, None], (2, members, cells_here))
    ones = ones.reshape(1, 2 * members, cells_here)
    upper = jnp.concatenate([pairs, ones, jnp.zeros_like(ones)], axis=0)
    lower = jnp.zeros((nvars + 2, 2, cells_here), f32).at[nvars + 1].set(masks)
    rhs = jnp.concatenate([upper, lower], axis=1)
    rhs = jnp.pad(rhs, ((0, 0), (0, LANES - used), (0, 0))).astype(bf16)
    row = lax.broadcasted_iota(jnp.int32, (TAIL, LANES), 0)
    lane = lax.broadcasted_iota(jnp.int32, (TAIL, LANES), 1)
    own_id = lax.axis_index("mem") * members_here + row
    another = (lane < 2 * members) & (lane % members != own_id)
    wanted = another | ((lane >= 2 * members) & (lane < used))
    keep = (wanted & (row < members_here)).astype(f32)
    fill = ((0, 0), (0, TAIL - members_here), (0, 0))
    own = jnp.pad(own_field.transpose(1, 0, 2), fill)
    off = jnp.pad(misfit.transpose(1, 0, 2), fill)
    d_preact, payload = backward(
        latent,
        in_weight,
        in_bias,
        out_weight,
        (sums, keep, own, off, rhs),
        entries,
        members,
        n_lat,
    )
    d_latent = down(d_preact, in_weight)
    scale = 1.0 / (members * cells_here * n_lat) ** 0.5
    received, d_latent = lax.optimization_barrier((exchange(payload, LAT), d_latent))
    payload = reduce_and_copy(received, n_mem, 1.0, "lat_sum")
    payload = reduce_and_copy(exchange(payload, "mem"), n_lat, scale, "mem_sum")
    return (d_latent, *spread_out(exchange(payload, LAT), width, hid, nvars))


def solution(mesh):
    n_mem, n_lat, n_rep = (mesh.shape[a] for a in ("mem", "lat", "rep"))
    split = Mesh(
        mesh.devices.reshape(n_mem, n_lat // 8, 2, 4, n_rep), ("mem", "band", "yl", "x", "rep")
    )
    placed = (P(("rep", "mem"), LAT, None), P(), P(), P(), P(), P("rep", LAT), P(LAT))
    return jax.shard_map(
        local,
        mesh=split,
        in_specs=placed,
        out_specs=(
            P(("rep", "mem"), LAT, None),
            P("rep", None),
            P("rep", None),
            P("rep"),
            P("rep"),
        ),
        check_vma=False,
    )
```
